32 devices in a mesh: lat: 4 (over y, core), lon: 8 (over z, x).
Axes of the slice: x: 2, y: 2, z: 4, core: 2. Of those that a mesh axis runs over, the one named last changes fastest.
Arguments:
- transport: float32 [4, 36, 128, 1024], P(None, None, 'lat', 'lon'), may hold values from 0.03 to 0.24
- mixing: float32 [35, 128, 1024], P(None, 'lat', 'lon'), may hold values from 0.05 to 5
- trajectory: bfloat16 [4, 3, 36, 128, 1024], P(None, None, None, 'lat', 'lon'), may hold values from -6 to 6
- kernel_table: float32 [64, 36], replicated, may hold values from 0 to 0.5
- track_tile: int32 [4, 16384, 1], P(None, ('lat', 'lon')), may hold values from 0 to 31; in each aligned block of 512 rows (0 to 511, 512 to 1023, ..., all dimensions but the last counted through in order) at most 32 rows name the same one
- sound_cell: int32 [4, 16384], P(None, ('lat', 'lon')), may hold values from 0 to 4095
- kernel_index: int32 [4, 16384], P(None, ('lat', 'lon')), may hold values from 0 to 63
- observed: float32 [4, 3, 16384], P(None, None, ('lat', 'lon')), may hold values from -8 to 8
- precision: float32 [4, 16384], P(None, ('lat', 'lon')), may hold values from 0.3 to 3
Outputs:
- adjoint_field: float32 [3, 36, 128, 1024], P(None, None, 'lat', 'lon')
- flux_grad: float32 [3, 128, 1024], P(None, 'lat', 'lon')
The draws below stay inside these ranges and needn't reach their ends.
Inputs may be any that keep to these rules, and one draw needn't show every extreme that they name: `track_tile`: within one step, the soundings held by one device name any one tile at most 32 times, and some device names some tile exactly 32 times.
All inputs are finite; a program needn't handle non-finite values.
Results may differ from the reference program's by a relative error of at most 0.0003.
Values may be sent and summed in bfloat16 or wider, within the bound.
A program may use at most 128 MiB of HBM per device.

```python
import math
import jax
import jax.numpy as jnp
import numpy as np

TRACERS = 3
LEV = 36
NKER = 64
STEPS = 4
LATC = 32
LONC = 128
SND_DEV = 512
NTILES = 32
CAP = 32
NLAT = 128
NLON = 1024
SOUNDINGS = 16384
N_LON = 8


def place_ends(values, rng, smallest, largest):
    index_at = [jax.random.randint(jax.random.fold_in(rng, axis), (), 0, length) for axis, length in enumerate(values.shape)]
    widest = values.shape.index(max(values.shape))
    next_to = index_at[:widest] + [(index_at[widest] + 1) % values.shape[widest]] + index_at[widest + 1:]
    return values.at[tuple(index_at)].set(smallest).at[tuple(next_to)].set(largest)


def levels(stream_key, dims, shards, low, high):
    loudness, own = 1.0, jax.random.fold_in(stream_key, 6)
    for position, blocks in shards:
        draws = jnp.exp(jax.random.uniform(jax.random.fold_in(own, position), (blocks,), jnp.float32, low / len(shards), high / len(shards)))
        loudness = loudness * jnp.repeat(draws, dims[position] // blocks).reshape([-1 if axis == position else 1 for axis in range(len(dims))])
    return loudness


def routed_block(key, own, number, rows, count, top, limit, lean):
    order = jax.random.permutation(key, count)
    heavy_load, ordinary = shares(count, rows * top, limit, lean, True), shares(count, rows * top, limit, lean, False)
    places = jnp.arange(count)

    def named(sizes, rotation):
        used = int((sizes > 0).sum())
        fixed = max(1, used // 4)
        shifted = fixed + (places - fixed + rotation * (used - fixed)) % max(1, count - fixed)
        return jnp.zeros((count,), jnp.int32).at[order[jnp.where(places < fixed, places, shifted)]].set(jnp.asarray(sizes, jnp.int32))

    sizes = jnp.where(number % 4 == 0, named(heavy_load, number // 4), named(ordinary, number - number // 4 - 1))
    mixed = jax.random.permutation(jax.random.fold_in(own, 3), count)
    donor, taker = mixed[0:count // 2 * 2:2], mixed[1:count // 2 * 2:2]
    room = jnp.minimum(sizes[donor] - 1, limit - sizes[taker]) // 2
    room = jnp.where((donor == order[0]) | (taker == order[0]) | (sizes[taker] == 0), 0, jnp.maximum(room, 0))
    shifted = jax.random.randint(jax.random.fold_in(own, 4), (count // 2,), 0, 1 << 20) % (room + 1)
    sizes = sizes.at[donor].add(-shifted).at[taker].add(shifted)
    members = jnp.searchsorted(jnp.cumsum(sizes), jnp.arange(rows * top), side="right").astype(jnp.int32)
    table = members.reshape(top, rows).T
    table = table[jax.random.permutation(jax.random.fold_in(own, 1), rows)]
    rotation = jax.random.randint(jax.random.fold_in(own, 2), (rows, 1), 0, top)
    return jnp.take_along_axis(table, (jnp.arange(top)[None, :] + rotation) % top, axis=1)


def shares(amount, total, most, slope, full):
    loads = [(1 << 20) // math.isqrt(grade ** slope) + 1 for grade in range(1, amount + 1)]
    largest = most if full else min(most, max(-(-total // amount), total * loads[0] // sum(loads)))
    least = 1 if total - largest >= amount - 1 else 0
    holding, spare = [largest] + [least] * (amount - 1), total - largest - least * (amount - 1)
    while spare > 0:
        candidates = [i for i in range(1, amount) if holding[i] < largest] or [i for i in range(1, amount) if holding[i] < most]
        whole, remaining = sum([loads[i] for i in candidates]), spare
        for i in candidates:
            extra = min(most - holding[i], max(1, remaining * loads[i] // whole), spare)
            holding[i] = holding[i] + extra
            spare = spare - extra
    return np.array(holding)


def bell_draw(own_key, extent, width, reach, cuts=(), dtype=jnp.bfloat16):
    values = jax.random.normal(own_key, extent, jnp.float32) * width
    if len(cuts) > 0:
        values = levels(own_key, extent, cuts, -0.22, 0.18) * values
    return jnp.clip(values, min=-reach, max=reach).astype(dtype)


def setup_inputs(seed: int = 0) -> dict:
    keys = jax.random.split(jax.random.key(seed), 10)
    transport = jnp.clip(0.03 + 0.21 * jax.random.uniform(keys[0], (4, LEV, NLAT, NLON), jnp.float32) ** levels(keys[0], (4, LEV, NLAT, NLON), ((2, 4), (3, 8)), -0.2, 0.2), 0.03, 0.24)
    mixing = jnp.clip(jnp.exp(math.log(5.0) - 4.6051702 * jax.random.uniform(keys[1], (LEV - 1, NLAT, NLON), jnp.float32) ** levels(keys[1], (LEV - 1, NLAT, NLON), ((1, 4), (2, 8)), -0.2, 0.2)), 0.05, 5.0)
    trajectory = bell_draw(keys[2], (STEPS, TRACERS, LEV, NLAT, NLON), 1.0, 6.0, ((3, 4), (4, 8)))
    kernel_table = jnp.clip(jax.random.uniform(keys[3], (NKER, LEV), jnp.float32, 0.0, 0.5), 0.0, 0.5)
    track_tile_keys = jax.random.split(jax.random.fold_in(keys[4], 1), STEPS * SOUNDINGS // SND_DEV)
    track_tile_turns = jax.random.permutation(jax.random.fold_in(keys[4], 3), STEPS * SOUNDINGS // SND_DEV)
    track_tile = jax.vmap(lambda own, number: routed_block(jax.random.fold_in(keys[4], 2), own, number, SND_DEV, NTILES, 1, CAP, 2))(track_tile_keys, track_tile_turns).reshape((STEPS, SOUNDINGS, 1))
    sound_cell = place_ends(jax.random.randint(keys[5], (STEPS, SOUNDINGS), 0, LATC * LONC), jax.random.fold_in(keys[5], 1), 0, (LATC * LONC) - 1).astype(jnp.int32)
    kernel_index = place_ends(jax.random.randint(keys[6], (STEPS, SOUNDINGS), 0, NKER), jax.random.fold_in(keys[6], 1), 0, NKER - 1).astype(jnp.int32)
    observed = bell_draw(keys[7], (STEPS, TRACERS, SOUNDINGS), 2.0, 8.0, ((2, 32),), jnp.float32)
    precision = jnp.clip(jnp.exp(math.log(3.0) - 2.3025851 * jax.random.uniform(keys[8], (STEPS, SOUNDINGS), jnp.float32) ** levels(keys[8], (STEPS, SOUNDINGS), ((1, 32),), -0.2, 0.2)), 0.3, 3.0)
    return {"transport": transport, "mixing": mixing, "trajectory": trajectory, "kernel_table": kernel_table, "track_tile": track_tile, "sound_cell": sound_cell, "kernel_index": kernel_index, "observed": observed, "precision": precision}


def vertical_setup(mixing):
    layers = mixing.shape[0] + 1
    diag_list = []
    for height in range(layers):
        diag_entry = jnp.ones_like(mixing[0])
        if height > 0:
            diag_entry = diag_entry + mixing[height - 1]
        if height < layers - 1:
            diag_entry = diag_entry + mixing[height]
        diag_list.append(diag_entry)
    inverse = [1.0 / diag_list[0]]
    upper_terms = [-mixing[0] * inverse[0]]
    for height in range(1, layers):
        denom_val = diag_list[height] + mixing[height - 1] * upper_terms[height - 1]
        inverse.append(1.0 / denom_val)
        if height < layers - 1:
            upper_terms.append(-mixing[height] * inverse[height])
    return upper_terms, inverse


def vertical_solve(field, mixing, upper_terms, inverse):
    layers = field.shape[1]
    forward = [field[:, 0] * inverse[0]]
    for height in range(1, layers):
        forward.append((field[:, height] + mixing[height - 1] * forward[height - 1]) * inverse[height])
    result = [forward[layers - 1]]
    for height in range(layers - 2, -1, -1):
        result.append(forward[height] - upper_terms[height] * result[-1])
    return jnp.stack(result[::-1], axis=1)


def horizontal(field, transport):
    center = 1.0 - transport[0] - transport[1] - transport[2] - transport[3]
    east_term = jnp.roll(transport[0] * field, 1, axis=-1)
    west_term = jnp.roll(transport[1] * field, -1, axis=-1)
    north_val = transport[2] * field
    south_val = transport[3] * field
    zero_row = jnp.zeros_like(north_val[..., :1, :])
    north_term = jnp.concatenate([zero_row, north_val[..., :-1, :]], axis=-2)
    south_term = jnp.concatenate([south_val[..., 1:, :], zero_row], axis=-2)
    return center * field + east_term + west_term + north_term + south_term


def reference(transport, mixing, trajectory, kernel_table, track_tile, sound_cell, kernel_index, observed, precision):
    tiles = track_tile[..., 0]
    grid_row = (tiles // N_LON) * LATC + sound_cell // LONC
    grid_col = (tiles % N_LON) * LONC + sound_cell % LONC
    column_of = (grid_row * NLON + grid_col).astype(jnp.int32)
    upper_terms, inverse = vertical_setup(mixing)
    adjoint = jnp.zeros((TRACERS, LEV, NLAT, NLON), jnp.float32)
    flux = jnp.zeros((TRACERS, NLAT, NLON), jnp.float32)
    for step_no in range(STEPS - 1, -1, -1):
        flat_bg = trajectory[step_no].reshape(TRACERS, LEV, NLAT * NLON)
        sampled = jnp.take(flat_bg, column_of[step_no], axis=2).astype(jnp.float32)
        weights = kernel_table[kernel_index[step_no]].T
        model = jnp.sum(weights[None] * sampled, axis=1)
        scaled = (model - observed[step_no]) * precision[step_no][None, :]
        force = (weights[None] * scaled[:, None, :]).reshape(TRACERS * LEV, -1)
        forcing = jnp.zeros((TRACERS * LEV, NLAT * NLON), jnp.float32).at[:, column_of[step_no]].add(force)
        adjoint = adjoint + forcing.reshape(TRACERS, LEV, NLAT, NLON)
        adjoint = horizontal(vertical_solve(adjoint, mixing, upper_terms, inverse), transport)
        flux = flux + adjoint[:, 0]
    return adjoint, flux
```

```python
import functools

import jax
import jax.numpy as jnp
from jax import lax
from jax.experimental import pallas as pl
from jax.experimental.pallas import tpu as pltpu
from jax.sharding import PartitionSpec as P

F32 = jnp.float32
BF16 = jnp.bfloat16
MESH = pl.DeviceIdType.MESH
FIELDS = 8
GROUP = 12


def parts(values, count):
    out = []
    for _ in range(count):
        part = values.astype(BF16).astype(F32)
        out.append(part)
        values = values - part
    return out


def pack_kernel(lon_count, cap, half, cols, tile_ref, cell_ref, index_ref, obs_ref, prec_ref, out_ref):
    steps, count, _ = tile_ref.shape
    tile_count = out_ref.shape[0]
    me = lax.axis_index("lat") * lon_count + lax.axis_index("lon")
    base = lax.rem(me, 128 // cap) * cap
    col_bits = cols.bit_length() - 1
    half_bits = half.bit_length() - 1
    row_id = lax.broadcasted_iota(jnp.int32, (count, count), 0)
    col_id = lax.broadcasted_iota(jnp.int32, (count, count), 1)
    before = (col_id < row_id).astype(F32).astype(BF16)
    lane_id = lax.broadcasted_iota(jnp.int32, (count, 128), 1)
    wide = 1024
    wide_id = lax.broadcasted_iota(jnp.int32, (count, wide), 1)
    for step in range(steps):
        tile = tile_ref[step]
        named = (lane_id == tile).astype(F32)
        ahead = jnp.dot(before, named.astype(BF16), preferred_element_type=F32)
        rank = jnp.sum(ahead * named, axis=1, keepdims=True).astype(jnp.int32)
        lane = tile * 128 + base + rank
        cell = cell_ref[pl.ds(step, 1), :]
        row = lax.shift_right_logical(cell, col_bits)
        place = lax.shift_right_logical(row, half_bits) * cols + (cell & (cols - 1)) + 1
        values = jnp.concatenate(
            [
                place.astype(F32),
                (row & (half - 1)).astype(F32),
                index_ref[pl.ds(step, 1), :].astype(F32),
                prec_ref[pl.ds(step, 1), :],
                obs_ref[step],
                jnp.zeros((1, count), F32),
            ],
            axis=0,
        )
        split = jnp.concatenate(parts(values, 3), axis=0).astype(BF16)
        for chunk in range(tile_count * 128 // wide):
            pick = (wide_id + chunk * wide == lane).astype(F32).astype(BF16)
            got = jnp.dot(split, pick, preferred_element_type=F32)
            got = got[:FIELDS] + got[FIELDS : 2 * FIELDS] + got[2 * FIELDS :]
            for part in range(wide // 128):
                out_ref[chunk * (wide // 128) + part, pl.ds(step * FIELDS, FIELDS), :] = got[
                    :, part * 128 : (part + 1) * 128
                ]


def window_kernel(
    lat_count,
    lon_count,
    got_ref,
    table_ref,
    transport_ref,
    mixing_ref,
    trajectory_ref,
    adjoint_ref,
    flux_ref,
    slots,
    weights,
    pieces,
    place_one,
    forcing,
    upper,
    inverse,
    center,
    row_out,
    row_in,
    col_out,
    col_in,
    send_sem,
    recv_sem,
):
    tracers, layers, rows, cols = adjoint_ref.shape
    steps = trajectory_ref.shape[0]
    half = rows // 2
    slot_count = slots.shape[1]
    lat = lax.axis_index("lat")
    lon = lax.axis_index("lon")
    east = lax.rem(lon + 1, lon_count)
    west = lax.rem(lon + lon_count - 1, lon_count)
    has_north = lat > 0
    has_south = lat < lat_count - 1

    barrier = pltpu.get_barrier_semaphore()
    for side in (east, west):
        pl.semaphore_signal(barrier, inc=1, device_id=(lat, side), device_id_type=MESH)

    @pl.when(has_north)
    def _():
        pl.semaphore_signal(barrier, inc=1, device_id=(lat - 1, lon), device_id_type=MESH)

    @pl.when(has_south)
    def _():
        pl.semaphore_signal(barrier, inc=1, device_id=(lat + 1, lon), device_id_type=MESH)

    @pl.when(jnp.logical_not(has_north))
    def _():
        row_in[:, 0] = jnp.zeros((steps, tracers, layers, cols), F32)

    @pl.when(jnp.logical_not(has_south))
    def _():
        row_in[:, 1] = jnp.zeros((steps, tracers, layers, cols), F32)

    per = got_ref.shape[0] * 128 // slot_count
    for group in range(slot_count // 128):
        total = got_ref[group * per]
        for member in range(1, per):
            total = total + got_ref[group * per + member]
        slots[:, group * 128 : (group + 1) * 128] = total

    den = 1.0 + mixing_ref[0]
    inv = 1.0 / den
    inverse[0] = inv
    upper[0] = -mixing_ref[0] * inv

    def setup(k, up):
        low = mixing_ref[k - 1]
        high = mixing_ref[k]
        inv = 1.0 / ((1.0 + low + high) + low * up)
        inverse[k] = inv
        up = -high * inv
        upper[k] = up
        return up

    up = lax.fori_loop(1, layers - 1, setup, upper[0])
    low = mixing_ref[layers - 2]
    inverse[layers - 1] = 1.0 / ((1.0 + low) + low * up)

    def middle(k, _):
        center[k] = (
            1.0 - transport_ref[0, k] - transport_ref[1, k] - transport_ref[2, k] - transport_ref[3, k]
        )
        return 0

    lax.fori_loop(0, layers, middle, 0)

    groups = layers // GROUP
    table_parts = [part.astype(BF16) for part in parts(table_ref[...], 3)]

    def observe(step):
        field = slots[step * FIELDS : (step + 1) * FIELDS, :]
        place_id = lax.broadcasted_iota(jnp.int32, (2 * cols, slot_count), 0)
        place_one[...] = (place_id == field[0:1].astype(jnp.int32) - 1).astype(F32).astype(BF16)
        half_id = lax.broadcasted_iota(jnp.int32, (half, slot_count), 0)
        mask = (half_id == field[1:2].astype(jnp.int32)).astype(F32)
        mask_short = mask.astype(BF16)
        kernel_id = lax.broadcasted_iota(jnp.int32, (table_ref.shape[1], slot_count), 0)
        kernel_one = (kernel_id == field[2:3].astype(jnp.int32)).astype(F32).astype(BF16)
        looked = [jnp.dot(part, kernel_one, preferred_element_type=F32) for part in table_parts]
        weights[...] = looked[0] + looked[1] + looked[2]

        def tracer(t, _):
            total = jnp.zeros((half, slot_count), F32)
            for group in range(groups):
                first = group * GROUP
                lhs = jnp.concatenate(
                    [
                        trajectory_ref[step, t, first : first + GROUP, :half, :].reshape(GROUP * half, cols),
                        trajectory_ref[step, t, first : first + GROUP, half:, :].reshape(GROUP * half, cols),
                    ],
                    axis=1,
                )
                sampled = jnp.dot(lhs, place_one[...], preferred_element_type=F32)
                for k in range(GROUP):
                    total = total + sampled[k * half : (k + 1) * half] * weights[first + k : first + k + 1, :]
            model = jnp.sum(total * mask, axis=0, keepdims=True)
            seen = slots[pl.ds(step * FIELDS + 4 + t, 1), :]
            scaled = (model - seen) * field[3:4]
            force = weights[...] * scaled
            big, small = parts(force, 2)
            pieces[0] = big
            pieces[1] = small
            for group in range(groups):
                first = group * GROUP
                placed = None
                for part in range(2):
                    lines = [
                        jnp.broadcast_to(
                            pieces[part, first + k : first + k + 1, :], (half, slot_count)
                        ).astype(BF16)
                        * mask_short
                        for k in range(GROUP)
                    ]
                    piece = lax.dot_general(
                        jnp.concatenate(lines, axis=0),
                        place_one[...],
                        (((1,), (1,)), ((), ())),
                        preferred_element_type=F32,
                    )
                    placed = piece if placed is None else placed + piece
                forcing[t, first : first + GROUP, :half, :] = placed[:, :cols].reshape(GROUP, half, cols)
                forcing[t, first : first + GROUP, half:, :] = placed[:, cols:].reshape(GROUP, half, cols)
            return 0

        lax.fori_loop(0, tracers, tracer, 0)

    lane = lax.broadcasted_iota(jnp.int32, (rows, cols), 1)
    line = lax.broadcasted_iota(jnp.int32, (rows, cols), 0)
    edge_pair = (lane == 0) | (lane == cols - 1)

    def vertical(first_step):
        def load(k):
            return forcing[:, k] if first_step else adjoint_ref[:, k] + forcing[:, k]

        d = load(0) * inverse[0]
        forcing[:, 0] = d

        def down(k, d):
            d = (load(k) + mixing_ref[k - 1] * d) * inverse[k]
            forcing[:, k] = d
            return d

        x = lax.fori_loop(1, layers, down, d, unroll=5)

        def back(i, x):
            k = layers - 2 - i
            x = forcing[:, k] - upper[k] * x
            forcing[:, k] = x
            return x

        lax.fori_loop(0, layers - 1, back, x, unroll=5)

    def pack(step):
        for t in range(tracers):
            def level(k, held):
                x = forcing[t, k]
                eastward = pltpu.roll(transport_ref[0, k] * x, 1, 1)
                westward = pltpu.roll(transport_ref[1, k] * x, cols - 1, 1)
                inner = center[k] * x + jnp.where(lane == 0, 0.0, eastward)
                inner = inner + jnp.where(lane == cols - 1, 0.0, westward)
                south = transport_ref[2, k] * x
                north = transport_ref[3, k] * x
                row_out[step, 0, t, pl.ds(k, 1), :] = north[0:1]
                row_out[step, 1, t, pl.ds(k, 1), :] = south[rows - 1 : rows]
                inner = inner + jnp.where(line == 0, 0.0, pltpu.roll(south, 1, 0))
                inner = inner + jnp.where(line == rows - 1, 0.0, pltpu.roll(north, rows - 1, 0))
                adjoint_ref[t, k] = inner
                both = pltpu.roll(jnp.where(lane == 0, eastward, westward), 2 * k, 1)
                here = (lane == 2 * k) | (lane == lax.rem(2 * k + cols - 1, cols))
                return jnp.where(here, both, held)

            col_out[step, t] = lax.fori_loop(0, layers, level, jnp.zeros((rows, cols), F32), unroll=4)

    def copies(step):
        north = pltpu.make_async_remote_copy(
            src_ref=row_out.at[step, 0], dst_ref=row_in.at[step, 1],
            send_sem=send_sem.at[step, 0], recv_sem=recv_sem.at[step, 1],
            device_id=(lat - 1, lon), device_id_type=MESH,
        )
        south = pltpu.make_async_remote_copy(
            src_ref=row_out.at[step, 1], dst_ref=row_in.at[step, 0],
            send_sem=send_sem.at[step, 1], recv_sem=recv_sem.at[step, 0],
            device_id=(lat + 1, lon), device_id_type=MESH,
        )
        to_east = pltpu.make_async_remote_copy(
            src_ref=col_out.at[step], dst_ref=col_in.at[step, 0],
            send_sem=send_sem.at[step, 2], recv_sem=recv_sem.at[step, 2],
            device_id=(lat, east), device_id_type=MESH,
        )
        to_west = pltpu.make_async_remote_copy(
            src_ref=col_out.at[step], dst_ref=col_in.at[step, 1],
            send_sem=send_sem.at[step, 3], recv_sem=recv_sem.at[step, 3],
            device_id=(lat, west), device_id_type=MESH,
        )
        return north, south, to_east, to_west

    def finish(step):
        for t in range(tracers):
            held = jnp.where((lane & 1) == 0, col_in[step, 0, t], col_in[step, 1, t])

            def level(k, _):
                shift = lax.rem(cols - 2 * k, cols)
                side = jnp.where(edge_pair, pltpu.roll(held, shift, 1), 0.0)
                top = jnp.where(line == 0, row_in[step, 0, t, pl.ds(k, 1), :], 0.0)
                bottom = jnp.where(line == rows - 1, row_in[step, 1, t, pl.ds(k, 1), :], 0.0)
                adjoint_ref[t, k] = adjoint_ref[t, k] + side + (top + bottom)
                return 0

            lax.fori_loop(0, layers, level, 0, unroll=4)

    count = 2 + has_north.astype(jnp.int32) + has_south.astype(jnp.int32)
    pl.semaphore_wait(barrier, count)

    observe(steps - 1)
    for step in range(steps - 1, -1, -1):
        vertical(step == steps - 1)
        pack(step)
        north, south, to_east, to_west = copies(step)
        to_east.start()
        to_west.start()

        @pl.when(has_north)
        def _():
            north.start()

        @pl.when(has_south)
        def _():
            south.start()

        if step > 0:
            observe(step - 1)

        to_east.wait()
        to_west.wait()

        @pl.when(has_north)
        def _():
            north.wait_send()
            south.wait_recv()

        @pl.when(has_south)
        def _():
            south.wait_send()
            north.wait_recv()

        finish(step)
        flux_ref[...] = adjoint_ref[:, 0] if step == steps - 1 else flux_ref[...] + adjoint_ref[:, 0]


def body(
    lat_count,
    lon_count,
    transport,
    mixing,
    trajectory,
    kernel_table,
    track_tile,
    sound_cell,
    kernel_index,
    observed,
    precision,
):
    tile_count = lat_count * lon_count
    steps, count, _ = track_tile.shape
    cap = max(2, 2 * count // tile_count)
    _, tracers, layers, rows, cols = trajectory.shape
    vmem = pl.BlockSpec(memory_space=pltpu.VMEM)
    packed = pl.pallas_call(
        functools.partial(pack_kernel, lon_count, cap, rows // 2, cols),
        out_shape=jax.ShapeDtypeStruct((tile_count, steps * FIELDS, 128), F32),
        in_specs=[vmem] * 5,
        out_specs=vmem,
        compiler_params=pltpu.CompilerParams(vmem_limit_bytes=40 << 20),
    )(track_tile, sound_cell, kernel_index, observed, precision)
    got = lax.all_to_all(packed, ("lat", "lon"), split_axis=0, concat_axis=0, tiled=True)
    slot_count = tile_count * cap
    field = (tracers, layers, rows, cols)
    return pl.pallas_call(
        functools.partial(window_kernel, lat_count, lon_count),
        out_shape=(jax.ShapeDtypeStruct(field, F32), jax.ShapeDtypeStruct((tracers, rows, cols), F32)),
        in_specs=[vmem] * 5,
        out_specs=(vmem, vmem),
        scratch_shapes=[
            pltpu.VMEM((steps * FIELDS, slot_count), F32),
            pltpu.VMEM((layers, slot_count), F32),
            pltpu.VMEM((2, layers, slot_count), F32),
            pltpu.VMEM((2 * cols, slot_count), BF16),
            pltpu.VMEM(field, F32),
            pltpu.VMEM((layers, rows, cols), F32),
            pltpu.VMEM((layers, rows, cols), F32),
            pltpu.VMEM((layers, rows, cols), F32),
            pltpu.VMEM((steps, 2, tracers, layers, cols), F32),
            pltpu.VMEM((steps, 2, tracers, layers, cols), F32),
            pltpu.VMEM((steps, tracers, rows, cols), F32),
            pltpu.VMEM((steps, 2, tracers, rows, cols), F32),
            pltpu.SemaphoreType.DMA((steps, 4)),
            pltpu.SemaphoreType.DMA((steps, 4)),
        ],
        compiler_params=pltpu.CompilerParams(
            collective_id=0, has_side_effects=True, vmem_limit_bytes=48 << 20
        ),
    )(got, kernel_table.T, transport, mixing, trajectory)


def solution(mesh):
    return jax.shard_map(
        functools.partial(body, mesh.shape["lat"], mesh.shape["lon"]),
        mesh=mesh,
        in_specs=(
            P(None, None, "lat", "lon"),
            P(None, "lat", "lon"),
            P(None, None, None, "lat", "lon"),
            P(),
            P(None, ("lat", "lon"), None),
            P(None, ("lat", "lon")),
            P(None, ("lat", "lon")),
            P(None, None, ("lat", "lon")),
            P(None, ("lat", "lon")),
        ),
        out_specs=(P(None, None, "lat", "lon"), P(None, "lat", "lon")),
        check_vma=False,
    )
```

```python
import functools

import jax
import jax.numpy as jnp
from jax import lax
from jax.experimental import pallas as pl
from jax.experimental.pallas import tpu as pltpu
from jax.sharding import PartitionSpec as P

F32 = jnp.float32
BF16 = jnp.bfloat16
MESH = pl.DeviceIdType.MESH
FIELDS = 8


def parts(values, count):
    out = []
    for _ in range(count):
        part = values.astype(BF16).astype(F32)
        out.append(part)
        values = values - part
    return out


def pack_kernel(cap, half, cols, tile_ref, cell_ref, index_ref, obs_ref, prec_ref, out_ref):
    steps, count = tile_ref.shape
    tile_count = out_ref.shape[0]
    slot_count = tile_count * cap
    col_bits = cols.bit_length() - 1
    half_bits = half.bit_length() - 1
    row_id = lax.broadcasted_iota(jnp.int32, (count, count), 0)
    col_id = lax.broadcasted_iota(jnp.int32, (count, count), 1)
    before = (row_id < col_id).astype(F32).astype(BF16)
    tile_id = lax.broadcasted_iota(jnp.int32, (tile_count, count), 0)
    slot_id = lax.broadcasted_iota(jnp.int32, (count, slot_count), 1)
    lane = lax.broadcasted_iota(jnp.int32, (FIELDS, 128), 1)
    slots = []
    for step in range(steps):
        tile = tile_ref[pl.ds(step, 1), :]
        named = (tile_id == tile).astype(F32)
        ahead = jnp.dot(named.astype(BF16), before, preferred_element_type=F32)
        rank = jnp.sum(ahead * named, axis=0, keepdims=True)
        slots.append((tile * cap).astype(F32) + rank)
    slots.append(jnp.zeros((8 - steps, count), F32))
    slot_columns = jnp.concatenate(slots, axis=0).T.astype(jnp.int32)
    blocks = [jnp.zeros((FIELDS, 128), F32)] * tile_count
    for step in range(steps):
        cell = cell_ref[pl.ds(step, 1), :]
        row = lax.shift_right_logical(cell, col_bits)
        place = lax.shift_right_logical(row, half_bits) * cols + (cell & (cols - 1)) + 1
        values = jnp.concatenate(
            [
                place.astype(F32),
                (row & (half - 1)).astype(F32),
                index_ref[pl.ds(step, 1), :].astype(F32),
                prec_ref[pl.ds(step, 1), :],
                obs_ref[step],
                jnp.zeros((1, count), F32),
            ],
            axis=0,
        )
        split = jnp.concatenate(parts(values, 3), axis=0).astype(BF16)
        pick = (slot_id == slot_columns[:, step : step + 1]).astype(F32).astype(BF16)
        got = jnp.dot(split, pick, preferred_element_type=F32)
        got = got[:FIELDS] + got[FIELDS : 2 * FIELDS] + got[2 * FIELDS :]
        here = (lane >= step * cap) & (lane < (step + 1) * cap)
        for tile in range(tile_count):
            first = tile * cap // 128 * 128
            piece = got[:, first : first + 128]
            shift = (step * cap + first - tile * cap) % 128
            if shift:
                piece = pltpu.roll(piece, shift, 1)
            blocks[tile] = jnp.where(here, piece, blocks[tile])
    for tile in range(tile_count):
        out_ref[tile] = blocks[tile]


def window_kernel(
    lat_count,
    lon_count,
    got_ref,
    table_ref,
    transport_ref,
    mixing_ref,
    trajectory_ref,
    adjoint_ref,
    flux_ref,
    slots,
    weights,
    pieces,
    place_one,
    place_turned,
    masked,
    forcing,
    upper,
    inverse,
    center,
    row_out,
    row_in,
    col_out,
    col_in,
    send_sem,
    recv_sem,
):
    tracers, layers, rows, cols = adjoint_ref.shape
    steps = trajectory_ref.shape[0]
    half = rows // 2
    slot_count = slots.shape[1]
    lat = lax.axis_index("lat")
    lon = lax.axis_index("lon")
    east = lax.rem(lon + 1, lon_count)
    west = lax.rem(lon + lon_count - 1, lon_count)
    has_north = lat > 0
    has_south = lat < lat_count - 1

    barrier = pltpu.get_barrier_semaphore()
    for side in (east, west):
        pl.semaphore_signal(barrier, inc=1, device_id=(lat, side), device_id_type=MESH)

    @pl.when(has_north)
    def _():
        pl.semaphore_signal(barrier, inc=1, device_id=(lat - 1, lon), device_id_type=MESH)

    @pl.when(has_south)
    def _():
        pl.semaphore_signal(barrier, inc=1, device_id=(lat + 1, lon), device_id_type=MESH)

    @pl.when(jnp.logical_not(has_north))
    def _():
        row_in[:, 0] = jnp.zeros((steps, tracers, layers, cols), F32)

    @pl.when(jnp.logical_not(has_south))
    def _():
        row_in[:, 1] = jnp.zeros((steps, tracers, layers, cols), F32)

    per = got_ref.shape[0] * 128 // slot_count
    cap = 128 // per
    slot_lane = lax.broadcasted_iota(jnp.int32, (FIELDS, 128), 1)
    for group in range(slot_count // 128):
        for step in range(steps):
            total = jnp.zeros((FIELDS, 128), F32)
            for member in range(per):
                block = got_ref[group * per + member]
                shift = (member - step) * cap % 128
                if shift:
                    block = pltpu.roll(block, shift, 1)
                here = (slot_lane >= member * cap) & (slot_lane < (member + 1) * cap)
                total = jnp.where(here, block, total)
            slots[step * FIELDS : (step + 1) * FIELDS, group * 128 : (group + 1) * 128] = total

    den = 1.0 + mixing_ref[0]
    inv = 1.0 / den
    inverse[0] = inv
    upper[0] = -mixing_ref[0] * inv

    def setup(k, up):
        low = mixing_ref[k - 1]
        high = mixing_ref[k]
        inv = 1.0 / ((1.0 + low + high) + low * up)
        inverse[k] = inv
        up = -high * inv
        upper[k] = up
        return up

    up = lax.fori_loop(1, layers - 1, setup, upper[0])
    low = mixing_ref[layers - 2]
    inverse[layers - 1] = 1.0 / ((1.0 + low) + low * up)

    def middle(k, _):
        center[k] = (
            1.0 - transport_ref[0, k] - transport_ref[1, k] - transport_ref[2, k] - transport_ref[3, k]
        )
        return 0

    lax.fori_loop(0, layers, middle, 0)

    table_parts = [part.astype(BF16) for part in parts(table_ref[...], 3)]
    channel = layers * half

    def observe(step):
        field = slots[step * FIELDS : (step + 1) * FIELDS, :]
        place_id = lax.broadcasted_iota(jnp.int32, (2 * cols, slot_count), 0)
        one = (place_id == field[0:1].astype(jnp.int32) - 1).astype(F32).astype(BF16)
        place_one[...] = one
        place_turned[...] = one.T
        half_id = lax.broadcasted_iota(jnp.int32, (half, slot_count), 0)
        mask = (half_id == field[1:2].astype(jnp.int32)).astype(F32)
        mask_short = mask.astype(BF16)
        kernel_id = lax.broadcasted_iota(jnp.int32, (table_ref.shape[1], slot_count), 0)
        kernel_one = (kernel_id == field[2:3].astype(jnp.int32)).astype(F32).astype(BF16)
        looked = [jnp.dot(part, kernel_one, preferred_element_type=F32) for part in table_parts]
        weights[...] = looked[0] + looked[1] + looked[2]

        for t in range(tracers):
            lhs = jnp.concatenate(
                [
                    trajectory_ref[step, t, :, :half, :].reshape(channel, cols),
                    trajectory_ref[step, t, :, half:, :].reshape(channel, cols),
                ],
                axis=1,
            )
            sampled = jnp.dot(lhs, place_one[...], preferred_element_type=F32)
            total = jnp.zeros((half, slot_count), F32)
            for k in range(layers):
                total = total + sampled[k * half : (k + 1) * half] * weights[k : k + 1, :]
            model = jnp.sum(total * mask, axis=0, keepdims=True)
            scaled = (model - field[4 + t : 5 + t]) * field[3:4]
            big, small = parts(weights[...] * scaled, 2)
            pieces[t, 0] = big
            pieces[t, 1] = small
            for part in range(2):
                for k in range(layers):
                    first = part * channel + k * half
                    line = jnp.broadcast_to(pieces[t, part, k : k + 1, :], (half, slot_count))
                    masked[t, first : first + half, :] = line.astype(BF16) * mask_short
            placed = jnp.dot(masked[t], place_turned[...], preferred_element_type=F32)
            placed = placed[:channel] + placed[channel:]
            forcing[t, :, :half, :] = placed[:, :cols].reshape(layers, half, cols)
            forcing[t, :, half:, :] = placed[:, cols:].reshape(layers, half, cols)

    lane = lax.broadcasted_iota(jnp.int32, (rows, cols), 1)
    line = lax.broadcasted_iota(jnp.int32, (rows, cols), 0)
    edge_pair = (lane == 0) | (lane == cols - 1)

    def vertical(first_step):
        def load(k):
            return forcing[:, k] if first_step else adjoint_ref[:, k] + forcing[:, k]

        d = load(0) * inverse[0]
        forcing[:, 0] = d

        def down(k, d):
            d = (load(k) + mixing_ref[k - 1] * d) * inverse[k]
            forcing[:, k] = d
            return d

        x = lax.fori_loop(1, layers, down, d, unroll=5)

        def back(i, x):
            k = layers - 2 - i
            x = forcing[:, k] - upper[k] * x
            forcing[:, k] = x
            return x

        lax.fori_loop(0, layers - 1, back, x, unroll=5)

    def pack(step):
        for t in range(tracers):
            def level(k, held):
                x = forcing[t, k]
                eastward = pltpu.roll(transport_ref[0, k] * x, 1, 1)
                westward = pltpu.roll(transport_ref[1, k] * x, cols - 1, 1)
                inner = center[k] * x + jnp.where(lane == 0, 0.0, eastward)
                inner = inner + jnp.where(lane == cols - 1, 0.0, westward)
                south = transport_ref[2, k] * x
                north = transport_ref[3, k] * x
                row_out[step, 0, t, pl.ds(k, 1), :] = north[0:1]
                row_out[step, 1, t, pl.ds(k, 1), :] = south[rows - 1 : rows]
                inner = inner + jnp.where(line == 0, 0.0, pltpu.roll(south, 1, 0))
                inner = inner + jnp.where(line == rows - 1, 0.0, pltpu.roll(north, rows - 1, 0))
                adjoint_ref[t, k] = inner
                both = pltpu.roll(jnp.where(lane == 0, eastward, westward), 2 * k, 1)
                here = (lane == 2 * k) | (lane == lax.rem(2 * k + cols - 1, cols))
                return jnp.where(here, both, held)

            col_out[step, t] = lax.fori_loop(0, layers, level, jnp.zeros((rows, cols), F32), unroll=4)

    def copies(step):
        north = pltpu.make_async_remote_copy(
            src_ref=row_out.at[step, 0], dst_ref=row_in.at[step, 1],
            send_sem=send_sem.at[step, 0], recv_sem=recv_sem.at[step, 1],
            device_id=(lat - 1, lon), device_id_type=MESH,
        )
        south = pltpu.make_async_remote_copy(
            src_ref=row_out.at[step, 1], dst_ref=row_in.at[step, 0],
            send_sem=send_sem.at[step, 1], recv_sem=recv_sem.at[step, 0],
            device_id=(lat + 1, lon), device_id_type=MESH,
        )
        to_east = pltpu.make_async_remote_copy(
            src_ref=col_out.at[step], dst_ref=col_in.at[step, 0],
            send_sem=send_sem.at[step, 2], recv_sem=recv_sem.at[step, 2],
            device_id=(lat, east), device_id_type=MESH,
        )
        to_west = pltpu.make_async_remote_copy(
            src_ref=col_out.at[step], dst_ref=col_in.at[step, 1],
            send_sem=send_sem.at[step, 3], recv_sem=recv_sem.at[step, 3],
            device_id=(lat, west), device_id_type=MESH,
        )
        return north, south, to_east, to_west

    def finish(step):
        for t in range(tracers):
            held = jnp.where((lane & 1) == 0, col_in[step, 0, t], col_in[step, 1, t])

            def level(k, _):
                shift = lax.rem(cols - 2 * k, cols)
                side = jnp.where(edge_pair, pltpu.roll(held, shift, 1), 0.0)
                top = jnp.where(line == 0, row_in[step, 0, t, pl.ds(k, 1), :], 0.0)
                bottom = jnp.where(line == rows - 1, row_in[step, 1, t, pl.ds(k, 1), :], 0.0)
                adjoint_ref[t, k] = adjoint_ref[t, k] + side + (top + bottom)
                return 0

            lax.fori_loop(0, layers, level, 0, unroll=4)

    count = 2 + has_north.astype(jnp.int32) + has_south.astype(jnp.int32)
    pl.semaphore_wait(barrier, count)

    observe(steps - 1)
    for step in range(steps - 1, -1, -1):
        vertical(step == steps - 1)
        pack(step)
        north, south, to_east, to_west = copies(step)
        to_east.start()
        to_west.start()

        @pl.when(has_north)
        def _():
            north.start()

        @pl.when(has_south)
        def _():
            south.start()

        if step > 0:
            observe(step - 1)

        to_east.wait()
        to_west.wait()

        @pl.when(has_north)
        def _():
            north.wait_send()
            south.wait_recv()

        @pl.when(has_south)
        def _():
            south.wait_send()
            north.wait_recv()

        finish(step)
        flux_ref[...] = adjoint_ref[:, 0] if step == steps - 1 else flux_ref[...] + adjoint_ref[:, 0]


def body(
    lat_count,
    lon_count,
    transport,
    mixing,
    trajectory,
    kernel_table,
    track_tile,
    sound_cell,
    kernel_index,
    observed,
    precision,
):
    tile_count = lat_count * lon_count
    steps, count, _ = track_tile.shape
    cap = max(2, 2 * count // tile_count)
    _, tracers, layers, rows, cols = trajectory.shape
    vmem = pl.BlockSpec(memory_space=pltpu.VMEM)
    packed = pl.pallas_call(
        functools.partial(pack_kernel, cap, rows // 2, cols),
        out_shape=jax.ShapeDtypeStruct((tile_count, FIELDS, 128), F32),
        in_specs=[vmem] * 5,
        out_specs=vmem,
        compiler_params=pltpu.CompilerParams(vmem_limit_bytes=40 << 20),
    )(track_tile[:, :, 0], sound_cell, kernel_index, observed, precision)
    got = lax.all_to_all(packed, ("lat", "lon"), split_axis=0, concat_axis=0, tiled=True)
    slot_count = tile_count * cap
    field = (tracers, layers, rows, cols)
    return pl.pallas_call(
        functools.partial(window_kernel, lat_count, lon_count),
        out_shape=(jax.ShapeDtypeStruct(field, F32), jax.ShapeDtypeStruct((tracers, rows, cols), F32)),
        in_specs=[vmem] * 5,
        out_specs=(vmem, vmem),
        scratch_shapes=[
            pltpu.VMEM((steps * FIELDS, slot_count), F32),
            pltpu.VMEM((layers, slot_count), F32),
            pltpu.VMEM((tracers, 2, layers, slot_count), F32),
            pltpu.VMEM((2 * cols, slot_count), BF16),
            pltpu.VMEM((slot_count, 2 * cols), BF16),
            pltpu.VMEM((tracers, layers * rows, slot_count), BF16),
            pltpu.VMEM(field, F32),
            pltpu.VMEM((layers, rows, cols), F32),
            pltpu.VMEM((layers, rows, cols), F32),
            pltpu.VMEM((layers, rows, cols), F32),
            pltpu.VMEM((steps, 2, tracers, layers, cols), F32),
            pltpu.VMEM((steps, 2, tracers, layers, cols), F32),
            pltpu.VMEM((steps, tracers, rows, cols), F32),
            pltpu.VMEM((steps, 2, tracers, rows, cols), F32),
            pltpu.SemaphoreType.DMA((steps, 4)),
            pltpu.SemaphoreType.DMA((steps, 4)),
        ],
        compiler_params=pltpu.CompilerParams(
            collective_id=0, has_side_effects=True, vmem_limit_bytes=48 << 20
        ),
    )(got, kernel_table.T, transport, mixing, trajectory)


def solution(mesh):
    return jax.shard_map(
        functools.partial(body, mesh.shape["lat"], mesh.shape["lon"]),
        mesh=mesh,
        in_specs=(
            P(None, None, "lat", "lon"),
            P(None, "lat", "lon"),
            P(None, None, None, "lat", "lon"),
            P(),
            P(None, ("lat", "lon"), None),
            P(None, ("lat", "lon")),
            P(None, ("lat", "lon")),
            P(None, None, ("lat", "lon")),
            P(None, ("lat", "lon")),
        ),
        out_specs=(P(None, None, "lat", "lon"), P(None, "lat", "lon")),
        check_vma=False,
    )
```

```python
import functools

import jax
import jax.numpy as jnp
from jax import lax
from jax.experimental import pallas as pl
from jax.experimental.pallas import tpu as pltpu
from jax.sharding import PartitionSpec as P

F32 = jnp.float32
BF16 = jnp.bfloat16
MESH = pl.DeviceIdType.MESH
FIELDS = 8


def parts(values, count):
    out = []
    for _ in range(count):
        part = values.astype(BF16).astype(F32)
        out.append(part)
        values = values - part
    return out


def pack_kernel(cap, half, cols, tile_ref, cell_ref, index_ref, obs_ref, prec_ref, out_ref):
    steps, count = tile_ref.shape
    tile_count = out_ref.shape[0]
    slot_count = tile_count * cap
    col_bits = cols.bit_length() - 1
    half_bits = half.bit_length() - 1
    row_id = lax.broadcasted_iota(jnp.int32, (count, count), 0)
    col_id = lax.broadcasted_iota(jnp.int32, (count, count), 1)
    before = (row_id < col_id).astype(F32).astype(BF16)
    tile_id = lax.broadcasted_iota(jnp.int32, (tile_count, count), 0)
    slot_id = lax.broadcasted_iota(jnp.int32, (count, slot_count), 1)
    lane = lax.broadcasted_iota(jnp.int32, (FIELDS, 128), 1)
    slots = []
    for step in range(steps):
        tile = tile_ref[pl.ds(step, 1), :]
        named = (tile_id == tile).astype(F32)
        ahead = jnp.dot(named.astype(BF16), before, preferred_element_type=F32)
        rank = jnp.sum(ahead * named, axis=0, keepdims=True)
        slots.append((tile * cap).astype(F32) + rank)
    slots.append(jnp.zeros((8 - steps, count), F32))
    slot_columns = jnp.concatenate(slots, axis=0).T.astype(jnp.int32)
    blocks = [jnp.zeros((FIELDS, 128), F32)] * tile_count
    for step in range(steps):
        cell = cell_ref[pl.ds(step, 1), :]
        row = lax.shift_right_logical(cell, col_bits)
        place = lax.shift_right_logical(row, half_bits) * cols + (cell & (cols - 1)) + 1
        values = jnp.concatenate(
            [
                place.astype(F32),
                (row & (half - 1)).astype(F32),
                index_ref[pl.ds(step, 1), :].astype(F32),
                prec_ref[pl.ds(step, 1), :],
                obs_ref[step],
                jnp.zeros((1, count), F32),
            ],
            axis=0,
        )
        split = jnp.concatenate(parts(values, 3), axis=0).astype(BF16)
        pick = (slot_id == slot_columns[:, step : step + 1]).astype(F32).astype(BF16)
        got = jnp.dot(split, pick, preferred_element_type=F32)
        got = got[:FIELDS] + got[FIELDS : 2 * FIELDS] + got[2 * FIELDS :]
        here = (lane >= step * cap) & (lane < (step + 1) * cap)
        for tile in range(tile_count):
            first = tile * cap // 128 * 128
            piece = got[:, first : first + 128]
            shift = (step * cap + first - tile * cap) % 128
            if shift:
                piece = pltpu.roll(piece, shift, 1)
            blocks[tile] = jnp.where(here, piece, blocks[tile])
    for tile in range(tile_count):
        out_ref[tile] = blocks[tile]


def window_kernel(
    lat_count,
    lon_count,
    got_ref,
    table_ref,
    transport_ref,
    mixing_ref,
    trajectory_ref,
    adjoint_ref,
    flux_ref,
    slots,
    weights,
    pieces,
    place_one,
    place_turned,
    masked,
    forcing,
    upper,
    inverse,
    center,
    row_out,
    row_in,
    col_out,
    col_in,
    sides,
    send_sem,
    recv_sem,
):
    tracers, layers, rows, cols = adjoint_ref.shape
    steps = trajectory_ref.shape[0]
    half = rows // 2
    slot_count = slots.shape[1]
    lat = lax.axis_index("lat")
    lon = lax.axis_index("lon")
    east = lax.rem(lon + 1, lon_count)
    west = lax.rem(lon + lon_count - 1, lon_count)
    has_north = lat > 0
    has_south = lat < lat_count - 1

    barrier = pltpu.get_barrier_semaphore()
    for side in (east, west):
        pl.semaphore_signal(barrier, inc=1, device_id=(lat, side), device_id_type=MESH)

    @pl.when(has_north)
    def _():
        pl.semaphore_signal(barrier, inc=1, device_id=(lat - 1, lon), device_id_type=MESH)

    @pl.when(has_south)
    def _():
        pl.semaphore_signal(barrier, inc=1, device_id=(lat + 1, lon), device_id_type=MESH)

    @pl.when(jnp.logical_not(has_north))
    def _():
        row_in[:, 0] = jnp.zeros((steps, tracers, layers, cols), F32)

    @pl.when(jnp.logical_not(has_south))
    def _():
        row_in[:, 1] = jnp.zeros((steps, tracers, layers, cols), F32)

    per = got_ref.shape[0] * 128 // slot_count
    cap = 128 // per
    slot_lane = lax.broadcasted_iota(jnp.int32, (FIELDS, 128), 1)
    for group in range(slot_count // 128):
        for step in range(steps):
            total = jnp.zeros((FIELDS, 128), F32)
            for member in range(per):
                block = got_ref[group * per + member]
                shift = (member - step) * cap % 128
                if shift:
                    block = pltpu.roll(block, shift, 1)
                here = (slot_lane >= member * cap) & (slot_lane < (member + 1) * cap)
                total = jnp.where(here, block, total)
            slots[step * FIELDS : (step + 1) * FIELDS, group * 128 : (group + 1) * 128] = total

    den = 1.0 + mixing_ref[0]
    inv = 1.0 / den
    inverse[0] = inv
    upper[0] = -mixing_ref[0] * inv

    def setup(k, up):
        low = mixing_ref[k - 1]
        high = mixing_ref[k]
        inv = 1.0 / ((1.0 + low + high) + low * up)
        inverse[k] = inv
        up = -high * inv
        upper[k] = up
        return up

    up = lax.fori_loop(1, layers - 1, setup, upper[0])
    low = mixing_ref[layers - 2]
    inverse[layers - 1] = 1.0 / ((1.0 + low) + low * up)

    def middle(k, _):
        center[k] = (
            1.0 - transport_ref[0, k] - transport_ref[1, k] - transport_ref[2, k] - transport_ref[3, k]
        )
        return 0

    lax.fori_loop(0, layers, middle, 0)

    table_parts = [part.astype(BF16) for part in parts(table_ref[...], 3)]
    channel = layers * half

    def observe(step):
        field = slots[step * FIELDS : (step + 1) * FIELDS, :]
        place_id = lax.broadcasted_iota(jnp.int32, (2 * cols, slot_count), 0)
        one = (place_id == field[0:1].astype(jnp.int32) - 1).astype(F32).astype(BF16)
        place_one[...] = one
        place_turned[...] = one.T
        half_id = lax.broadcasted_iota(jnp.int32, (half, slot_count), 0)
        mask = (half_id == field[1:2].astype(jnp.int32)).astype(F32)
        mask_short = mask.astype(BF16)
        kernel_id = lax.broadcasted_iota(jnp.int32, (table_ref.shape[1], slot_count), 0)
        kernel_one = (kernel_id == field[2:3].astype(jnp.int32)).astype(F32).astype(BF16)
        looked = [jnp.dot(part, kernel_one, preferred_element_type=F32) for part in table_parts]
        weights[...] = looked[0] + looked[1] + looked[2]

        for t in range(tracers):
            lhs = jnp.concatenate(
                [
                    trajectory_ref[step, t, :, :half, :].reshape(channel, cols),
                    trajectory_ref[step, t, :, half:, :].reshape(channel, cols),
                ],
                axis=1,
            )
            sampled = jnp.dot(lhs, place_one[...], preferred_element_type=F32)
            total = jnp.zeros((half, slot_count), F32)
            for k in range(layers):
                total = total + sampled[k * half : (k + 1) * half] * weights[k : k + 1, :]
            model = jnp.sum(total * mask, axis=0, keepdims=True)
            scaled = (model - field[4 + t : 5 + t]) * field[3:4]
            big, small = parts(weights[...] * scaled, 2)
            pieces[t, 0] = big
            pieces[t, 1] = small
            for part in range(2):
                for k in range(layers):
                    first = part * channel + k * half
                    line = jnp.broadcast_to(pieces[t, part, k : k + 1, :], (half, slot_count))
                    masked[t, first : first + half, :] = line.astype(BF16) * mask_short
            placed = jnp.dot(masked[t], place_turned[...], preferred_element_type=F32)
            placed = placed[:channel] + placed[channel:]
            forcing[t, :, :half, :] = placed[:, :cols].reshape(layers, half, cols)
            forcing[t, :, half:, :] = placed[:, cols:].reshape(layers, half, cols)

    lane = lax.broadcasted_iota(jnp.int32, (rows, cols), 1)
    line = lax.broadcasted_iota(jnp.int32, (rows, cols), 0)
    edge_pair = (lane == 0) | (lane == cols - 1)
    line_eight = lax.broadcasted_iota(jnp.int32, (8, cols), 0)
    upper[layers - 1] = jnp.zeros((rows, cols), F32)

    def merge(step):
        for t in range(tracers):
            from_east = pltpu.roll(col_in[step, 1, t], cols - 2, 1)
            sides[t] = jnp.where((lane & 1) == 0, col_in[step, 0, t], from_east)

    def arrived(step, t, k):
        side = jnp.where(edge_pair, pltpu.roll(sides[t], lax.rem(cols - 2 * k, cols), 1), 0.0)
        full = adjoint_ref[t, k] + side
        top = jnp.where(line_eight == 0, row_in[step, 0, t, pl.ds(k, 1), :], 0.0)
        bottom = jnp.where(line_eight == 7, row_in[step, 1, t, pl.ds(k, 1), :], 0.0)
        return jnp.concatenate([full[:8] + top, full[8 : rows - 8], full[rows - 8 :] + bottom], axis=0)

    def add_flux(t, value, first_step):
        flux_ref[t] = value if first_step else flux_ref[t] + value

    def sweep_up(step):
        first = step == steps - 1

        def load(t, k):
            return forcing[t, k] if first else arrived(step + 1, t, k) + forcing[t, k]

        start = []
        for t in range(tracers):
            value = forcing[t, 0]
            if not first:
                before = arrived(step + 1, t, 0)
                add_flux(t, before, step == steps - 2)
                value = value + before
            start.append(value * inverse[0])
            forcing[t, 0] = start[-1]

        def level(k, held):
            out = []
            for t in range(tracers):
                d = (load(t, k) + mixing_ref[k - 1] * held[t]) * inverse[k]
                forcing[t, k] = d
                out.append(d)
            return tuple(out)

        lax.fori_loop(1, layers, level, tuple(start), unroll=5)

    def sweep_down(step):
        def level(i, carry):
            k = layers - 1 - i
            xs, packed = carry
            new_xs, new_packed = [], []
            here = (lane == 2 * k) | (lane == 2 * k + 1)
            for t in range(tracers):
                x = forcing[t, k] - upper[k] * xs[t]
                eastward = transport_ref[0, k] * x
                westward = transport_ref[1, k] * x
                south = transport_ref[2, k] * x
                north = transport_ref[3, k] * x
                row_out[step, 0, t, pl.ds(k, 1), :] = north[0:1]
                row_out[step, 1, t, pl.ds(k, 1), :] = south[rows - 1 : rows]
                both = pltpu.roll(jnp.where(lane == cols - 1, eastward, westward), 2 * k + 1, 1)
                inner = center[k] * x + jnp.where(lane == 0, 0.0, pltpu.roll(eastward, 1, 1))
                inner = inner + jnp.where(lane == cols - 1, 0.0, pltpu.roll(westward, cols - 1, 1))
                inner = inner + jnp.where(line == 0, 0.0, pltpu.roll(south, 1, 0))
                inner = inner + jnp.where(line == rows - 1, 0.0, pltpu.roll(north, rows - 1, 0))
                adjoint_ref[t, k] = inner
                new_xs.append(x)
                new_packed.append(jnp.where(here, both, packed[t]))
            return tuple(new_xs), tuple(new_packed)

        zeros = (jnp.zeros((rows, cols), F32),) * tracers
        _, packed = lax.fori_loop(0, layers, level, (zeros, zeros), unroll=4)
        for t in range(tracers):
            col_out[step, t] = packed[t]

    def copies(step):
        north = pltpu.make_async_remote_copy(
            src_ref=row_out.at[step, 0], dst_ref=row_in.at[step, 1],
            send_sem=send_sem.at[step, 0], recv_sem=recv_sem.at[step, 1],
            device_id=(lat - 1, lon), device_id_type=MESH,
        )
        south = pltpu.make_async_remote_copy(
            src_ref=row_out.at[step, 1], dst_ref=row_in.at[step, 0],
            send_sem=send_sem.at[step, 1], recv_sem=recv_sem.at[step, 0],
            device_id=(lat + 1, lon), device_id_type=MESH,
        )
        to_east = pltpu.make_async_remote_copy(
            src_ref=col_out.at[step], dst_ref=col_in.at[step, 0],
            send_sem=send_sem.at[step, 2], recv_sem=recv_sem.at[step, 2],
            device_id=(lat, east), device_id_type=MESH,
        )
        to_west = pltpu.make_async_remote_copy(
            src_ref=col_out.at[step], dst_ref=col_in.at[step, 1],
            send_sem=send_sem.at[step, 3], recv_sem=recv_sem.at[step, 3],
            device_id=(lat, west), device_id_type=MESH,
        )
        return north, south, to_east, to_west

    def finish(step):
        for t in range(tracers):
            value = arrived(step, t, 0)
            adjoint_ref[t, 0] = value
            add_flux(t, value, step == steps - 1)

        def level(k, _):
            for t in range(tracers):
                adjoint_ref[t, k] = arrived(step, t, k)
            return 0

        lax.fori_loop(1, layers, level, 0, unroll=5)

    count = 2 + has_north.astype(jnp.int32) + has_south.astype(jnp.int32)
    pl.semaphore_wait(barrier, count)

    observe(steps - 1)
    for step in range(steps - 1, -1, -1):
        sweep_up(step)
        sweep_down(step)
        north, south, to_east, to_west = copies(step)
        to_east.start()
        to_west.start()

        @pl.when(has_north)
        def _():
            north.start()

        @pl.when(has_south)
        def _():
            south.start()

        if step > 0:
            observe(step - 1)

        to_east.wait()
        to_west.wait()

        @pl.when(has_north)
        def _():
            north.wait_send()
            south.wait_recv()

        @pl.when(has_south)
        def _():
            south.wait_send()
            north.wait_recv()

        merge(step)
    finish(0)


def body(
    lat_count,
    lon_count,
    transport,
    mixing,
    trajectory,
    kernel_table,
    track_tile,
    sound_cell,
    kernel_index,
    observed,
    precision,
):
    tile_count = lat_count * lon_count
    steps, count, _ = track_tile.shape
    cap = max(2, 2 * count // tile_count)
    _, tracers, layers, rows, cols = trajectory.shape
    vmem = pl.BlockSpec(memory_space=pltpu.VMEM)
    packed = pl.pallas_call(
        functools.partial(pack_kernel, cap, rows // 2, cols),
        out_shape=jax.ShapeDtypeStruct((tile_count, FIELDS, 128), F32),
        in_specs=[vmem] * 5,
        out_specs=vmem,
        compiler_params=pltpu.CompilerParams(vmem_limit_bytes=40 << 20),
    )(track_tile[:, :, 0], sound_cell, kernel_index, observed, precision)
    got = lax.all_to_all(packed, ("lat", "lon"), split_axis=0, concat_axis=0, tiled=True)
    slot_count = tile_count * cap
    field = (tracers, layers, rows, cols)
    return pl.pallas_call(
        functools.partial(window_kernel, lat_count, lon_count),
        out_shape=(jax.ShapeDtypeStruct(field, F32), jax.ShapeDtypeStruct((tracers, rows, cols), F32)),
        in_specs=[vmem] * 5,
        out_specs=(vmem, vmem),
        scratch_shapes=[
            pltpu.VMEM((steps * FIELDS, slot_count), F32),
            pltpu.VMEM((layers, slot_count), F32),
            pltpu.VMEM((tracers, 2, layers, slot_count), F32),
            pltpu.VMEM((2 * cols, slot_count), BF16),
            pltpu.VMEM((slot_count, 2 * cols), BF16),
            pltpu.VMEM((tracers, layers * rows, slot_count), BF16),
            pltpu.VMEM(field, F32),
            pltpu.VMEM((layers, rows, cols), F32),
            pltpu.VMEM((layers, rows, cols), F32),
            pltpu.VMEM((layers, rows, cols), F32),
            pltpu.VMEM((steps, 2, tracers, layers, cols), F32),
            pltpu.VMEM((steps, 2, tracers, layers, cols), F32),
            pltpu.VMEM((steps, tracers, rows, cols), F32),
            pltpu.VMEM((steps, 2, tracers, rows, cols), F32),
            pltpu.VMEM((tracers, rows, cols), F32),
            pltpu.SemaphoreType.DMA((steps, 4)),
            pltpu.SemaphoreType.DMA((steps, 4)),
        ],
        compiler_params=pltpu.CompilerParams(
            collective_id=0, has_side_effects=True, vmem_limit_bytes=48 << 20
        ),
    )(got, kernel_table.T, transport, mixing, trajectory)


def solution(mesh):
    return jax.shard_map(
        functools.partial(body, mesh.shape["lat"], mesh.shape["lon"]),
        mesh=mesh,
        in_specs=(
            P(None, None, "lat", "lon"),
            P(None, "lat", "lon"),
            P(None, None, None, "lat", "lon"),
            P(),
            P(None, ("lat", "lon"), None),
            P(None, ("lat", "lon")),
            P(None, ("lat", "lon")),
            P(None, None, ("lat", "lon")),
            P(None, ("lat", "lon")),
        ),
        out_specs=(P(None, None, "lat", "lon"), P(None, "lat", "lon")),
        check_vma=False,
    )
```

```python
import functools

import jax
import jax.numpy as jnp
from jax import lax
from jax.experimental import pallas as pl
from jax.experimental.pallas import tpu as pltpu
from jax.sharding import PartitionSpec as P

F32 = jnp.float32
BF16 = jnp.bfloat16
MESH = pl.DeviceIdType.MESH
FIELDS = 8


def parts(values, count):
    out = []
    for _ in range(count):
        part = values.astype(BF16).astype(F32)
        out.append(part)
        values = values - part
    return out


def pack_kernel(cap, half, cols, tile_ref, cell_ref, index_ref, obs_ref, prec_ref, out_ref):
    steps, count = tile_ref.shape
    tile_count = out_ref.shape[0]
    slot_count = tile_count * cap
    col_bits = cols.bit_length() - 1
    half_bits = half.bit_length() - 1
    row_id = lax.broadcasted_iota(jnp.int32, (count, count), 0)
    col_id = lax.broadcasted_iota(jnp.int32, (count, count), 1)
    before = (row_id < col_id).astype(F32).astype(BF16)
    tile_id = lax.broadcasted_iota(jnp.int32, (tile_count, count), 0)
    slot_id = lax.broadcasted_iota(jnp.int32, (count, slot_count), 1)
    lane = lax.broadcasted_iota(jnp.int32, (FIELDS, 128), 1)
    slots = []
    for step in range(steps):
        tile = tile_ref[pl.ds(step, 1), :]
        named = (tile_id == tile).astype(F32)
        ahead = jnp.dot(named.astype(BF16), before, preferred_element_type=F32)
        rank = jnp.sum(ahead * named, axis=0, keepdims=True)
        slots.append((tile * cap).astype(F32) + rank)
    slots.append(jnp.zeros((8 - steps, count), F32))
    slot_columns = jnp.concatenate(slots, axis=0).T.astype(jnp.int32)
    blocks = [jnp.zeros((FIELDS, 128), F32)] * tile_count
    for step in range(steps):
        cell = cell_ref[pl.ds(step, 1), :]
        row = lax.shift_right_logical(cell, col_bits)
        place = lax.shift_right_logical(row, half_bits) * cols + (cell & (cols - 1)) + 1
        values = jnp.concatenate(
            [
                place.astype(F32),
                (row & (half - 1)).astype(F32),
                index_ref[pl.ds(step, 1), :].astype(F32),
                prec_ref[pl.ds(step, 1), :],
                obs_ref[step],
                jnp.zeros((1, count), F32),
            ],
            axis=0,
        )
        split = jnp.concatenate(parts(values, 3), axis=0).astype(BF16)
        pick = (slot_id == slot_columns[:, step : step + 1]).astype(F32).astype(BF16)
        got = jnp.dot(split, pick, preferred_element_type=F32)
        got = got[:FIELDS] + got[FIELDS : 2 * FIELDS] + got[2 * FIELDS :]
        here = (lane >= step * cap) & (lane < (step + 1) * cap)
        for tile in range(tile_count):
            first = tile * cap // 128 * 128
            piece = got[:, first : first + 128]
            shift = (step * cap + first - tile * cap) % 128
            if shift:
                piece = pltpu.roll(piece, shift, 1)
            blocks[tile] = jnp.where(here, piece, blocks[tile])
    for tile in range(tile_count):
        out_ref[tile] = blocks[tile]


def window_kernel(
    lat_count,
    lon_count,
    packed_ref,
    table_ref,
    transport_ref,
    mixing_ref,
    trajectory_ref,
    adjoint_ref,
    flux_ref,
    got_ref,
    slots,
    weights,
    pieces,
    place_one,
    place_turned,
    masked,
    forcing,
    upper,
    inverse,
    center,
    row_out,
    row_in,
    col_out,
    col_in,
    sides,
    send_sem,
    recv_sem,
    out_sem,
    in_sem,
):
    tracers, layers, rows, cols = adjoint_ref.shape
    steps = trajectory_ref.shape[0]
    half = rows // 2
    slot_count = slots.shape[1]
    lat = lax.axis_index("lat")
    lon = lax.axis_index("lon")
    east = lax.rem(lon + 1, lon_count)
    west = lax.rem(lon + lon_count - 1, lon_count)
    has_north = lat > 0
    has_south = lat < lat_count - 1

    me = lat * lon_count + lon
    total_count = lat_count * lon_count

    def place_of(j):
        other = lax.rem(me + j, total_count)
        return other, (lax.div(other, lon_count), lax.rem(other, lon_count))

    barrier = pltpu.get_barrier_semaphore()

    def greet(j, _):
        pl.semaphore_signal(barrier, inc=1, device_id=place_of(j)[1], device_id_type=MESH)
        return 0

    lax.fori_loop(1, total_count, greet, 0)
    pl.semaphore_wait(barrier, total_count - 1)

    def send(j, _):
        other, place = place_of(j)
        pltpu.make_async_remote_copy(
            src_ref=packed_ref.at[other], dst_ref=got_ref.at[me],
            send_sem=out_sem.at[other], recv_sem=in_sem.at[me],
            device_id=place, device_id_type=MESH,
        ).start()
        return 0

    lax.fori_loop(1, total_count, send, 0)
    got_ref[me] = packed_ref[me]

    @pl.when(jnp.logical_not(has_north))
    def _():
        row_in[:, 0] = jnp.zeros((steps, tracers, layers, cols), F32)

    @pl.when(jnp.logical_not(has_south))
    def _():
        row_in[:, 1] = jnp.zeros((steps, tracers, layers, cols), F32)

    den = 1.0 + mixing_ref[0]
    inv = 1.0 / den
    inverse[0] = inv
    upper[0] = -mixing_ref[0] * inv

    def setup(k, up):
        low = mixing_ref[k - 1]
        high = mixing_ref[k]
        inv = 1.0 / ((1.0 + low + high) + low * up)
        inverse[k] = inv
        up = -high * inv
        upper[k] = up
        return up

    up = lax.fori_loop(1, layers - 1, setup, upper[0])
    low = mixing_ref[layers - 2]
    inverse[layers - 1] = 1.0 / ((1.0 + low) + low * up)

    def middle(k, _):
        center[k] = (
            1.0 - transport_ref[0, k] - transport_ref[1, k] - transport_ref[2, k] - transport_ref[3, k]
        )
        return 0

    lax.fori_loop(0, layers, middle, 0)

    def settle(j, _):
        other, place = place_of(j)
        pltpu.make_async_remote_copy(
            src_ref=packed_ref.at[other], dst_ref=got_ref.at[other],
            send_sem=out_sem.at[other], recv_sem=in_sem.at[other],
            device_id=place, device_id_type=MESH,
        ).wait()
        return 0

    lax.fori_loop(1, total_count, settle, 0)

    per = got_ref.shape[0] * 128 // slot_count
    cap = 128 // per
    slot_lane = lax.broadcasted_iota(jnp.int32, (FIELDS, 128), 1)
    for group in range(slot_count // 128):
        for step in range(steps):
            total = jnp.zeros((FIELDS, 128), F32)
            for member in range(per):
                block = got_ref[group * per + member]
                shift = (member - step) * cap % 128
                if shift:
                    block = pltpu.roll(block, shift, 1)
                here = (slot_lane >= member * cap) & (slot_lane < (member + 1) * cap)
                total = jnp.where(here, block, total)
            slots[step * FIELDS : (step + 1) * FIELDS, group * 128 : (group + 1) * 128] = total

    table_parts = [part.astype(BF16) for part in parts(table_ref[...], 3)]
    channel = layers * half

    def observe(step):
        field = slots[step * FIELDS : (step + 1) * FIELDS, :]
        place_id = lax.broadcasted_iota(jnp.int32, (2 * cols, slot_count), 0)
        one = (place_id == field[0:1].astype(jnp.int32) - 1).astype(F32).astype(BF16)
        place_one[...] = one
        place_turned[...] = one.T
        half_id = lax.broadcasted_iota(jnp.int32, (half, slot_count), 0)
        mask = (half_id == field[1:2].astype(jnp.int32)).astype(F32)
        mask_short = mask.astype(BF16)
        kernel_id = lax.broadcasted_iota(jnp.int32, (table_ref.shape[1], slot_count), 0)
        kernel_one = (kernel_id == field[2:3].astype(jnp.int32)).astype(F32).astype(BF16)
        looked = [jnp.dot(part, kernel_one, preferred_element_type=F32) for part in table_parts]
        weights[...] = looked[0] + looked[1] + looked[2]

        for t in range(tracers):
            lhs = jnp.concatenate(
                [
                    trajectory_ref[step, t, :, :half, :].reshape(channel, cols),
                    trajectory_ref[step, t, :, half:, :].reshape(channel, cols),
                ],
                axis=1,
            )
            sampled = jnp.dot(lhs, place_one[...], preferred_element_type=F32)
            total = jnp.zeros((half, slot_count), F32)
            for k in range(layers):
                total = total + sampled[k * half : (k + 1) * half] * weights[k : k + 1, :]
            model = jnp.sum(total * mask, axis=0, keepdims=True)
            scaled = (model - field[4 + t : 5 + t]) * field[3:4]
            big, small = parts(weights[...] * scaled, 2)
            pieces[t, 0] = big
            pieces[t, 1] = small
            for part in range(2):
                for k in range(layers):
                    first = part * channel + k * half
                    line = jnp.broadcast_to(pieces[t, part, k : k + 1, :], (half, slot_count))
                    masked[t, first : first + half, :] = line.astype(BF16) * mask_short
            placed = jnp.dot(masked[t], place_turned[...], preferred_element_type=F32)
            placed = placed[:channel] + placed[channel:]
            forcing[t, :, :half, :] = placed[:, :cols].reshape(layers, half, cols)
            forcing[t, :, half:, :] = placed[:, cols:].reshape(layers, half, cols)

    lane = lax.broadcasted_iota(jnp.int32, (rows, cols), 1)
    line = lax.broadcasted_iota(jnp.int32, (rows, cols), 0)
    edge_pair = (lane == 0) | (lane == cols - 1)
    line_eight = lax.broadcasted_iota(jnp.int32, (8, cols), 0)
    upper[layers - 1] = jnp.zeros((rows, cols), F32)

    def merge(step):
        for t in range(tracers):
            from_east = pltpu.roll(col_in[step, 1, t], cols - 2, 1)
            sides[t] = jnp.where((lane & 1) == 0, col_in[step, 0, t], from_east)

    def arrived(step, t, k):
        side = jnp.where(edge_pair, pltpu.roll(sides[t], lax.rem(cols - 2 * k, cols), 1), 0.0)
        full = adjoint_ref[t, k] + side
        top = jnp.where(line_eight == 0, row_in[step, 0, t, pl.ds(k, 1), :], 0.0)
        bottom = jnp.where(line_eight == 7, row_in[step, 1, t, pl.ds(k, 1), :], 0.0)
        return jnp.concatenate([full[:8] + top, full[8 : rows - 8], full[rows - 8 :] + bottom], axis=0)

    def add_flux(t, value, first_step):
        flux_ref[t] = value if first_step else flux_ref[t] + value

    def sweep_up(step):
        first = step == steps - 1

        def load(t, k):
            return forcing[t, k] if first else arrived(step + 1, t, k) + forcing[t, k]

        start = []
        for t in range(tracers):
            value = forcing[t, 0]
            if not first:
                before = arrived(step + 1, t, 0)
                add_flux(t, before, step == steps - 2)
                value = value + before
            start.append(value * inverse[0])
            forcing[t, 0] = start[-1]

        def level(k, held):
            out = []
            for t in range(tracers):
                d = (load(t, k) + mixing_ref[k - 1] * held[t]) * inverse[k]
                forcing[t, k] = d
                out.append(d)
            return tuple(out)

        lax.fori_loop(1, layers, level, tuple(start), unroll=5)

    def sweep_down(step):
        def level(i, carry):
            k = layers - 1 - i
            xs, packed = carry
            new_xs, new_packed = [], []
            here = (lane == 2 * k) | (lane == 2 * k + 1)
            for t in range(tracers):
                x = forcing[t, k] - upper[k] * xs[t]
                eastward = transport_ref[0, k] * x
                westward = transport_ref[1, k] * x
                south = transport_ref[2, k] * x
                north = transport_ref[3, k] * x
                row_out[step, 0, t, pl.ds(k, 1), :] = north[0:1]
                row_out[step, 1, t, pl.ds(k, 1), :] = south[rows - 1 : rows]
                both = pltpu.roll(jnp.where(lane == cols - 1, eastward, westward), 2 * k + 1, 1)
                inner = center[k] * x + jnp.where(lane == 0, 0.0, pltpu.roll(eastward, 1, 1))
                inner = inner + jnp.where(lane == cols - 1, 0.0, pltpu.roll(westward, cols - 1, 1))
                inner = inner + jnp.where(line == 0, 0.0, pltpu.roll(south, 1, 0))
                inner = inner + jnp.where(line == rows - 1, 0.0, pltpu.roll(north, rows - 1, 0))
                adjoint_ref[t, k] = inner
                new_xs.append(x)
                new_packed.append(jnp.where(here, both, packed[t]))
            return tuple(new_xs), tuple(new_packed)

        zeros = (jnp.zeros((rows, cols), F32),) * tracers
        _, packed = lax.fori_loop(0, layers, level, (zeros, zeros), unroll=4)
        for t in range(tracers):
            col_out[step, t] = packed[t]

    def copies(step):
        north = pltpu.make_async_remote_copy(
            src_ref=row_out.at[step, 0], dst_ref=row_in.at[step, 1],
            send_sem=send_sem.at[step, 0], recv_sem=recv_sem.at[step, 1],
            device_id=(lat - 1, lon), device_id_type=MESH,
        )
        south = pltpu.make_async_remote_copy(
            src_ref=row_out.at[step, 1], dst_ref=row_in.at[step, 0],
            send_sem=send_sem.at[step, 1], recv_sem=recv_sem.at[step, 0],
            device_id=(lat + 1, lon), device_id_type=MESH,
        )
        to_east = pltpu.make_async_remote_copy(
            src_ref=col_out.at[step], dst_ref=col_in.at[step, 0],
            send_sem=send_sem.at[step, 2], recv_sem=recv_sem.at[step, 2],
            device_id=(lat, east), device_id_type=MESH,
        )
        to_west = pltpu.make_async_remote_copy(
            src_ref=col_out.at[step], dst_ref=col_in.at[step, 1],
            send_sem=send_sem.at[step, 3], recv_sem=recv_sem.at[step, 3],
            device_id=(lat, west), device_id_type=MESH,
        )
        return north, south, to_east, to_west

    def finish(step):
        for t in range(tracers):
            value = arrived(step, t, 0)
            adjoint_ref[t, 0] = value
            add_flux(t, value, step == steps - 1)

        def level(k, _):
            for t in range(tracers):
                adjoint_ref[t, k] = arrived(step, t, k)
            return 0

        lax.fori_loop(1, layers, level, 0, unroll=5)

    observe(steps - 1)
    for step in range(steps - 1, -1, -1):
        sweep_up(step)
        sweep_down(step)
        north, south, to_east, to_west = copies(step)
        to_east.start()
        to_west.start()

        @pl.when(has_north)
        def _():
            north.start()

        @pl.when(has_south)
        def _():
            south.start()

        if step > 0:
            observe(step - 1)

        to_east.wait()
        to_west.wait()

        @pl.when(has_north)
        def _():
            north.wait_send()
            south.wait_recv()

        @pl.when(has_south)
        def _():
            south.wait_send()
            north.wait_recv()

        merge(step)
    finish(0)


def body(
    lat_count,
    lon_count,
    transport,
    mixing,
    trajectory,
    kernel_table,
    track_tile,
    sound_cell,
    kernel_index,
    observed,
    precision,
):
    tile_count = lat_count * lon_count
    steps, count, _ = track_tile.shape
    cap = max(2, 2 * count // tile_count)
    _, tracers, layers, rows, cols = trajectory.shape
    vmem = pl.BlockSpec(memory_space=pltpu.VMEM)
    packed = pl.pallas_call(
        functools.partial(pack_kernel, cap, rows // 2, cols),
        out_shape=jax.ShapeDtypeStruct((tile_count, FIELDS, 128), F32),
        in_specs=[vmem] * 5,
        out_specs=vmem,
        compiler_params=pltpu.CompilerParams(vmem_limit_bytes=40 << 20),
    )(track_tile[:, :, 0], sound_cell, kernel_index, observed, precision)
    slot_count = tile_count * cap
    field = (tracers, layers, rows, cols)
    return pl.pallas_call(
        functools.partial(window_kernel, lat_count, lon_count),
        out_shape=(jax.ShapeDtypeStruct(field, F32), jax.ShapeDtypeStruct((tracers, rows, cols), F32)),
        in_specs=[vmem] * 5,
        out_specs=(vmem, vmem),
        scratch_shapes=[
            pltpu.VMEM((tile_count, FIELDS, 128), F32),
            pltpu.VMEM((steps * FIELDS, slot_count), F32),
            pltpu.VMEM((layers, slot_count), F32),
            pltpu.VMEM((tracers, 2, layers, slot_count), F32),
            pltpu.VMEM((2 * cols, slot_count), BF16),
            pltpu.VMEM((slot_count, 2 * cols), BF16),
            pltpu.VMEM((tracers, layers * rows, slot_count), BF16),
            pltpu.VMEM(field, F32),
            pltpu.VMEM((layers, rows, cols), F32),
            pltpu.VMEM((layers, rows, cols), F32),
            pltpu.VMEM((layers, rows, cols), F32),
            pltpu.VMEM((steps, 2, tracers, layers, cols), F32),
            pltpu.VMEM((steps, 2, tracers, layers, cols), F32),
            pltpu.VMEM((steps, tracers, rows, cols), F32),
            pltpu.VMEM((steps, 2, tracers, rows, cols), F32),
            pltpu.VMEM((tracers, rows, cols), F32),
            pltpu.SemaphoreType.DMA((steps, 4)),
            pltpu.SemaphoreType.DMA((steps, 4)),
            pltpu.SemaphoreType.DMA((tile_count,)),
            pltpu.SemaphoreType.DMA((tile_count,)),
        ],
        compiler_params=pltpu.CompilerParams(
            collective_id=0, has_side_effects=True, vmem_limit_bytes=48 << 20
        ),
    )(packed, kernel_table.T, transport, mixing, trajectory)


def solution(mesh):
    return jax.shard_map(
        functools.partial(body, mesh.shape["lat"], mesh.shape["lon"]),
        mesh=mesh,
        in_specs=(
            P(None, None, "lat", "lon"),
            P(None, "lat", "lon"),
            P(None, None, None, "lat", "lon"),
            P(),
            P(None, ("lat", "lon"), None),
            P(None, ("lat", "lon")),
            P(None, ("lat", "lon")),
            P(None, None, ("lat", "lon")),
            P(None, ("lat", "lon")),
        ),
        out_specs=(P(None, None, "lat", "lon"), P(None, "lat", "lon")),
        check_vma=False,
    )
```
